128 devices in a mesh: seq: 32 (over z, x, core), mp: 4 (over y).
Axes of the slice: x: 4, y: 4, z: 4, core: 2. Of those that a mesh axis runs over, the one named last changes fastest.
Arguments:
- hidden_in: float32 [16384, 1024], P('seq'), may hold values from -6 to 6
- mix_gain: float32 [1024], replicated, may hold values from 0.1 to 1.9
- in_weight: bfloat16 [1024, 3, 1024], P(None, None, 'mp'), may hold values from -0.1875 to 0.1875
- conv_weight: float32 [3, 1024], P(None, 'mp'), may hold values from -3 to 3
- out_weight: bfloat16 [1024, 1024], P('mp'), may hold values from -0.1875 to 0.1875
- ffn_gain: float32 [1024], replicated, may hold values from 0.1 to 1.9
- gate_up_weight: bfloat16 [1024, 2, 4608], P(None, None, 'mp'), may hold values from -0.1875 to 0.1875
- down_weight: bfloat16 [4608, 1024], P('mp'), may hold values from -0.09375 to 0.09375
- seq_starts: int32 [32], P('seq'), may hold values from 1 to 512, as said below
- out_grad: float32 [16384, 1024], P('seq'), may hold values from -6 to 6
Outputs:
- hidden_out: float32 [16384, 1024], P('seq')
- hidden_grad: float32 [16384, 1024], P('seq')
- mix_gain_grad: float32 [1024], replicated
- in_weight_grad: float32 [1024, 3, 1024], P('seq', None, 'mp')
- conv_weight_grad: float32 [3, 1024], P(None, 'mp')
- out_weight_grad: float32 [1024, 1024], P('mp', 'seq')
- ffn_gain_grad: float32 [1024], replicated
- gate_up_grad: float32 [1024, 2, 4608], P('seq', None, 'mp')
- down_grad: float32 [4608, 1024], P('mp', 'seq')
The draws below stay inside these ranges and needn't reach their ends.
Inputs may be any that keep to these rules, and one draw needn't show every extreme that they name: seq_starts[0] lies in 1 to 256, the last entry in 256 to 511, and every other entry is 512: one sequence runs from inside the first slab to inside the last.
All inputs are finite; a program needn't handle non-finite values.
Results may differ from the reference program's by a relative error of at most 0.012.
Values may be sent and summed in bfloat16 or wider, within the bound.
No kernel may reach another device: no remote copies, remote signals or barrier semaphores. Data moves between devices by JAX's collectives and lax.ppermute only.
A program may use at most 128 MiB of HBM per device.

```python
import jax
import jax.numpy as jnp
from jax import lax

D = 1024
FF = 4608
TOK_DEV = 512
TOKENS = 16384
N_SEQ = 32


def draw_seq_starts(key, part):
    key = jax.random.fold_in(key, 11)
    first_key, last_key = jax.random.split(key)
    first_cut = jax.random.randint(first_key, (), 1, TOK_DEV // 2 + 1)
    last_cut = jax.random.randint(last_key, (), TOK_DEV // 2, TOK_DEV)
    places = jnp.arange(N_SEQ)
    return jnp.where(places == 0, first_cut, jnp.where(places == N_SEQ - 1, last_cut, TOK_DEV)).astype(jnp.int32)


def strengthened(drawn, stream_key, source, target, blocks, factor):
    def block_of(axis_at):
        return (jnp.arange(drawn.shape[axis_at]) // (drawn.shape[axis_at] // blocks)).reshape((-1,) + (1,) * (drawn.ndim - 1 - axis_at))

    first = jax.random.permutation(stream_key, blocks)[block_of(target)]
    far = (block_of(target) + blocks // 2) % blocks
    return jnp.where((block_of(source) == first) | (block_of(source) == far), factor * drawn, drawn)


def block_scale(own_key, dims, cuts, least, high):
    level = 1.0
    for axis_at, parts in cuts:
        steps = jax.random.uniform(jax.random.fold_in(jax.random.fold_in(own_key, 6), axis_at), (parts,), jnp.float32, least / len(cuts), high / len(cuts))
        level = level * jnp.repeat(jnp.exp(steps), dims[axis_at] // parts).reshape((-1,) + (1,) * (len(dims) - 1 - axis_at))
    return level


def normal_values(rng, shape, deviation, most, pieces=(), held_as=jnp.bfloat16):
    level = block_scale(rng, shape, pieces, -0.22, 0.18) if pieces else 1.0
    result = jax.random.normal(rng, shape, jnp.float32) * deviation * level
    return jnp.minimum(jnp.maximum(result, -most), most).astype(held_as)


def heavy_noise(own_key, dims, width, limit, cuts, heavy, kind=jnp.bfloat16):
    array = width * jax.random.normal(own_key, dims, jnp.float32)
    if cuts:
        array = array * block_scale(own_key, dims, cuts, -0.22, 0.18)
    return jnp.clip(strengthened(array, jax.random.fold_in(own_key, 3), *heavy), -limit, limit).astype(kind)


def setup_inputs(seed: int = 0) -> dict:
    seeds = jax.random.split(jax.random.key(seed), 11)
    return {
        "hidden_in": heavy_noise(seeds[0], (TOKENS, D), 1.0, 6.0, ((0, 32),), (0, 1, 32, 2.75), jnp.float32),
        "mix_gain": jnp.clip(1.0 + 0.18 * jax.random.normal(seeds[1], (D,), jnp.float32), 0.1, 1.9),
        "in_weight": normal_values(seeds[2], (D, 3, D), D ** -0.5, 0.1875, ((2, 4),)),
        "conv_weight": normal_values(seeds[3], (3, D), 0.6, 3.0, ((1, 4),), jnp.float32),
        "out_weight": normal_values(seeds[4], (D, D), D ** -0.5, 0.1875, ((0, 4),)),
        "ffn_gain": jnp.clip(1.0 + 0.18 * jax.random.normal(seeds[5], (D,), jnp.float32), 0.1, 1.9),
        "gate_up_weight": normal_values(seeds[6], (D, 2, FF), D ** -0.5, 0.1875, ((2, 4),)),
        "down_weight": normal_values(seeds[7], (FF, D), FF ** -0.5, 0.09375, ((0, 4),)),
        "seq_starts": draw_seq_starts(jax.random.fold_in(seeds[10], 71), 0),
        "out_grad": heavy_noise(seeds[9], (TOKENS, D), 1.0, 6.0, ((0, 32),), (0, 1, 32, 2.75), jnp.float32),
    }


EPS = 1e-05
HIGH = lax.Precision.HIGHEST

@jax.custom_vjp
def low(v):
    return lax.optimization_barrier(v.astype(jnp.bfloat16)).astype(jnp.float32)

@jax.custom_vjp
def low_back(v):
    return v

def low_keep(v):
    return (low(v), None)

def low_pass(kept, grad):
    return (grad,)

def back_keep(v):
    return (v, None)

def back_low(kept, grad):
    return (low(grad),)
low.defvjp(low_keep, low_pass)
low_back.defvjp(back_keep, back_low)

def rms_scale(values):
    return values * lax.rsqrt(lax.optimization_barrier(jnp.mean(values * values, axis=-1, keepdims=True)) + EPS)

def block_forward(hidden, mix_gain, in_weight, conv_weight, out_weight, ffn_gain, gate_up_weight, down_weight, keep_one, keep_two):
    normed = low(rms_scale(hidden) * mix_gain)
    project = low_back(jnp.einsum('td,dkc->tkc', normed, in_weight, precision=HIGH))
    mixed_in = low_back(low(project[:, 0] * project[:, 2]))
    zero_row = jnp.zeros((1, mixed_in.shape[1]), jnp.float32)
    back_one = jnp.concatenate([zero_row, mixed_in[:-1]], 0) * keep_one[:, None]
    back_two = jnp.concatenate([zero_row, zero_row, mixed_in[:-2]], 0) * keep_two[:, None]
    convolved = conv_weight[0] * back_two + conv_weight[1] * back_one + conv_weight[2] * mixed_in
    gated = low(project[:, 1] * convolved)
    branch = low_back(jnp.dot(gated, out_weight, precision=HIGH))
    middle = hidden + branch
    normed_two = low(rms_scale(middle) * ffn_gain)
    gate_up = low_back(jnp.einsum('td,dkf->tkf', normed_two, gate_up_weight, precision=HIGH))
    active = low(jax.nn.silu(gate_up[:, 0]) * gate_up[:, 1])
    return middle + low_back(jnp.dot(active, down_weight, precision=HIGH))

def reference(hidden_in, mix_gain, in_weight, conv_weight, out_weight, ffn_gain, gate_up_weight, down_weight, seq_starts, out_grad):
    within = (jnp.arange(TOKENS) % TOK_DEV).astype(jnp.int32)
    opens = (within == jnp.repeat(seq_starts, TOK_DEV).astype(jnp.int32)).astype(jnp.int32)
    before = jnp.concatenate([jnp.zeros((1,), jnp.int32), opens[:-1]])
    keep_one = (1 - opens).astype(jnp.float32)
    keep_two = ((1 - opens) * (1 - before)).astype(jnp.float32)

    def run(hidden, gain_a, weight_a, taps, weight_b, gain_b, weight_c, weight_d):
        return block_forward(hidden, gain_a, weight_a, taps, weight_b, gain_b, weight_c, weight_d, keep_one, keep_two)
    hidden_out, pullback = jax.vjp(run, hidden_in, mix_gain, in_weight.astype(jnp.float32), conv_weight, out_weight.astype(jnp.float32), ffn_gain, gate_up_weight.astype(jnp.float32), down_weight.astype(jnp.float32))
    grads = pullback(out_grad)
    return (hidden_out, grads[0], grads[1], grads[2], grads[3], grads[4], grads[5], grads[6], grads[7])
```

```python
import jax
import jax.numpy as jnp
from jax import lax
from jax.sharding import PartitionSpec as P

EPS = 1e-05
LOW = jnp.bfloat16
FULL = jnp.float32
MP = 4
X_DIM = 4
Z_DIM = 4


def ring_shift(size, by):
    return [(i, (i + by) % size) for i in range(size)]


def seq_index(z, x, core):
    return (z * X_DIM + x) * 2 + core


def seq_shift(dz, dx, flip):
    return [
        (
            seq_index(z, x, core),
            seq_index((z + dz) % Z_DIM, (x + dx) % X_DIM, core ^ flip),
        )
        for z in range(Z_DIM)
        for x in range(X_DIM)
        for core in range(2)
    ]


def slab_shift(value, by):
    devices = lax.axis_size("seq")
    pairs = [(i, i + by) for i in range(devices) if 0 <= i + by < devices]
    return lax.ppermute(value, "seq", pairs)


def dot(left, right, contract):
    return lax.dot_general(left, right, (contract, ((), ())), preferred_element_type=FULL)


def sum_rows(part):
    rows = part.shape[0] // MP
    total = part[:rows].astype(FULL)
    came = [
        lax.ppermute(part[o * rows : (o + 1) * rows], "mp", ring_shift(MP, o)) for o in (1, 3, 2)
    ]
    for value in came:
        total = total + value.astype(FULL)
    return total


def gather_rows(rows):
    came = {o: lax.ppermute(rows, "mp", ring_shift(MP, -o)) for o in (1, 3, 2)}
    return jnp.concatenate([rows, came[1], came[2], came[3]], axis=0)


def take(value, index, axis):
    return lax.dynamic_index_in_dim(value, index, axis, keepdims=False)


def scatter_sum(part, order):
    me = lax.axis_index("seq")
    core, x, z = me % 2, (me // 2) % X_DIM, me // (2 * X_DIM)
    cols = part.shape[1]
    part = part.reshape(Z_DIM, X_DIM, 2, -1, cols)
    came = lax.ppermute(take(part, 1 - core, 2), "seq", seq_shift(0, 0, 1))
    part = take(part, core, 2).astype(FULL) + came.astype(FULL)
    for name in order:
        mine, axis = (x, 1) if name == "x" else (z, 0)
        axis = min(axis, part.ndim - 3)
        total = take(part, mine, axis)
        low = part.astype(LOW)
        for o in (1, 3, 2):
            shift = seq_shift(0, o, 0) if name == "x" else seq_shift(o, 0, 0)
            came = lax.ppermute(take(low, (mine + o) % 4, axis), "seq", shift)
            total = total + came.astype(FULL)
        part = total
    return part


def norm_back(grad_unit, unit_rows, inv_rows):
    return inv_rows * (
        grad_unit - unit_rows * jnp.mean(grad_unit * unit_rows, axis=1, keepdims=True)
    )


def turn(value, by):
    rows = value.shape[0]
    return lax.dynamic_slice_in_dim(jnp.concatenate([value, value], 0), by, rows, 0)


def on_device(
    hidden_in,
    mix_gain,
    in_weight,
    conv_weight,
    out_weight,
    ffn_gain,
    gate_up_weight,
    down_weight,
    seq_starts,
    out_grad,
):
    rows, width = hidden_in.shape
    mine = rows // MP
    channels = conv_weight.shape[1]
    me = lax.axis_index("mp")
    start = me * mine
    place = (jnp.arange(rows, dtype=jnp.int32) + start) % rows
    opens = place == seq_starts[0]
    after_open = place == seq_starts[0] + 1
    keep_one = (1.0 - opens.astype(FULL))[:, None]
    keep_two = (1.0 - (opens | after_open).astype(FULL))[:, None]
    is_first = (place == 0)[:, None]
    is_second = (place == 1)[:, None]
    is_last = (place == rows - 1)[:, None]
    is_before_last = (place == rows - 2)[:, None]

    w_in = in_weight.reshape(width, -1)
    w_gu = gate_up_weight.reshape(width, -1)

    tail_in = slab_shift(hidden_in[rows - 8 :], 1)
    inv_tail = lax.rsqrt(jnp.mean(tail_in * tail_in, axis=1, keepdims=True) + EPS)
    tail_normed = (tail_in * inv_tail * mix_gain).astype(LOW)
    tail_project = dot(tail_normed, w_in, ((1,), (0,)))
    came_state = (
        (tail_project[:, :channels] * tail_project[:, 2 * channels :]).astype(LOW).astype(FULL)
    )
    came_two, came_one = came_state[6:7], came_state[7:8]

    hidden = turn(hidden_in, start)
    inv_first = lax.rsqrt(jnp.mean(hidden * hidden, axis=1, keepdims=True) + EPS)
    unit_first = hidden * inv_first
    normed = (unit_first * mix_gain).astype(LOW)
    project = dot(normed, w_in, ((1,), (0,)))
    b_part = project[:, :channels]
    c_part = project[:, channels : 2 * channels]
    x_part = project[:, 2 * channels :]
    mixed = (b_part * x_part).astype(LOW).astype(FULL)
    back_one = jnp.concatenate([mixed[-1:], mixed[:-1]], 0)
    back_two = jnp.concatenate([mixed[-2:], mixed[:-2]], 0)
    tap_one = jnp.where(is_first, came_one, back_one) * keep_one
    tap_two = jnp.where(is_first, came_two, jnp.where(is_second, came_one, back_two)) * keep_two
    convolved = conv_weight[0] * tap_two + conv_weight[1] * tap_one + conv_weight[2] * mixed
    gated = (c_part * convolved).astype(LOW)
    branch = sum_rows(dot(gated, out_weight, ((1,), (0,))).astype(LOW))
    middle = hidden[:mine] + branch
    inv_second = lax.rsqrt(jnp.mean(middle * middle, axis=1, keepdims=True) + EPS)
    unit_second = middle * inv_second
    normed_two = gather_rows((unit_second * ffn_gain).astype(LOW))

    out_grad_turned = turn(out_grad, start)
    grad_low = out_grad_turned.astype(LOW)
    grad_active = dot(grad_low, down_weight, ((1,), (1,)))
    gate_up = dot(normed_two, w_gu, ((1,), (0,)))
    hidden_units = down_weight.shape[0]
    gate_val = gate_up[:, :hidden_units]
    upper_val = gate_up[:, hidden_units:]
    sigma = jax.nn.sigmoid(gate_val)
    active = (gate_val * sigma * upper_val).astype(LOW)
    grad_gate = grad_active * upper_val * sigma * (1.0 + gate_val * (1.0 - sigma))
    grad_upper = grad_active * gate_val * sigma
    grad_gu = jnp.concatenate([grad_gate.astype(LOW), grad_upper.astype(LOW)], axis=1)
    grad_normed_two = sum_rows(dot(grad_gu, w_gu, ((1,), (1,))).astype(LOW))
    ffn_gain_part = jnp.sum(grad_normed_two * unit_second, axis=0)
    grad_middle = out_grad_turned[:mine] + norm_back(
        grad_normed_two * ffn_gain, unit_second, inv_second
    )
    ffn_rows = sum_rows(dot(active, down_weight, ((1,), (0,))).astype(LOW))
    hidden_out = turn(gather_rows((middle + ffn_rows).astype(LOW)), (rows - start) % rows)
    gate_up_part = dot(normed_two, grad_gu, ((0,), (0,))).astype(LOW)
    down_part = dot(grad_low, active, ((0,), (0,))).astype(LOW)
    gate_up_done = scatter_sum(gate_up_part, "xz")
    down_done = scatter_sum(down_part, "zx")

    grad_branch = gather_rows(grad_middle.astype(LOW))
    grad_gated = dot(grad_branch, out_weight, ((1,), (1,)))
    head = lax.dynamic_slice_in_dim(grad_branch, (rows - start) % rows, 8, 0)
    head_c = lax.dynamic_slice_in_dim(c_part, (rows - start) % rows, 8, 0)
    head_conv = dot(head, out_weight, ((1,), (1,))) * head_c
    first_open = seq_starts[0]
    head_one = (first_open != 0).astype(FULL)
    head_two = ((first_open != 0) & (first_open != 1)).astype(FULL)
    head_grad = jnp.concatenate(
        [
            conv_weight[0:1] * head_conv[0:1] * head_one,
            conv_weight[0:1] * head_conv[1:2] * head_two
            + conv_weight[1:2] * head_conv[0:1] * head_one,
        ],
        axis=0,
    )
    came_grad = slab_shift(head_grad, -1)
    grad_c = grad_gated * convolved
    grad_conv = grad_gated * c_part
    to_two = conv_weight[0] * grad_conv * keep_two
    to_one = conv_weight[1] * grad_conv * keep_one
    from_one = jnp.concatenate([to_one[1:], to_one[:1]], 0)
    from_two = jnp.concatenate([to_two[2:], to_two[:2]], 0)
    grad_mixed = (
        conv_weight[2] * grad_conv
        + jnp.where(is_last, came_grad[1:2], from_one)
        + jnp.where(is_last, 0.0, jnp.where(is_before_last, came_grad[0:1], from_two))
    )
    conv_part = jnp.stack(
        [
            jnp.sum(grad_conv * tap_two, axis=0),
            jnp.sum(grad_conv * tap_one, axis=0),
            jnp.sum(grad_conv * mixed, axis=0),
        ],
        axis=0,
    )
    grad_mixed = grad_mixed.astype(LOW).astype(FULL)
    grad_project = jnp.concatenate(
        [(grad_mixed * x_part).astype(LOW), grad_c.astype(LOW), (grad_mixed * b_part).astype(LOW)],
        axis=1,
    )
    grad_normed_part = dot(grad_project, w_in, ((1,), (1,)))
    mix_gain_part = jnp.sum(grad_normed_part * unit_first, axis=0)
    grad_normed = sum_rows(grad_normed_part.astype(LOW))
    hidden_grad = grad_middle + norm_back(
        grad_normed * mix_gain, unit_first[:mine], inv_first[:mine]
    )
    hidden_grad = turn(gather_rows(hidden_grad.astype(LOW)), (rows - start) % rows)
    in_out_part = jnp.concatenate(
        [
            dot(normed, grad_project, ((0,), (0,))).astype(LOW),
            dot(grad_branch, gated, ((0,), (0,))).astype(LOW),
        ],
        axis=1,
    )
    in_out_done = scatter_sum(in_out_part, "zx")
    mix_gain_grad, ffn_gain_grad = lax.psum((mix_gain_part, ffn_gain_part), ("seq", "mp"))
    conv_weight_grad = lax.psum(conv_part, "seq")
    local = in_out_done.shape[0]
    return (
        hidden_out.astype(FULL),
        hidden_grad.astype(FULL),
        mix_gain_grad,
        in_out_done[:, : 3 * channels].reshape(local, 3, channels),
        conv_weight_grad,
        in_out_done[:, 3 * channels :].T,
        ffn_gain_grad,
        gate_up_done.reshape(local, 2, hidden_units),
        down_done.T,
    )


def solution(mesh):
    placed = (
        P("seq", None),
        P(),
        P(None, None, "mp"),
        P(None, "mp"),
        P("mp", None),
        P(),
        P(None, None, "mp"),
        P("mp", None),
        P("seq"),
        P("seq", None),
    )
    return jax.shard_map(
        on_device,
        mesh=mesh,
        in_specs=placed,
        out_specs=(
            P("seq", None),
            P("seq", None),
            P(),
            P("seq", None, "mp"),
            P(None, "mp"),
            P("mp", "seq"),
            P(),
            P("seq", None, "mp"),
            P("mp", "seq"),
        ),
        check_vma=False,
    )
```

```python
import functools
import math

import jax
import jax.numpy as jnp
from jax import lax
from jax.experimental import pallas as pl
from jax.experimental.pallas import tpu as pltpu
from jax.sharding import PartitionSpec as P

EPS = 1e-05
LOW = jnp.bfloat16
FULL = jnp.float32
MP = 4
X_DIM = 4
ORDER = (0, 1, 3, 2)
Z_DIM = 4


def ring_shift(size, by):
    return [(i, (i + by) % size) for i in range(size)]


def seq_index(z, x, core):
    return (z * X_DIM + x) * 2 + core


def seq_shift(dz, dx, flip):
    return [
        (
            seq_index(z, x, core),
            seq_index((z + dz) % Z_DIM, (x + dx) % X_DIM, core ^ flip),
        )
        for z in range(Z_DIM)
        for x in range(X_DIM)
        for core in range(2)
    ]


def slab_shift(value, by):
    devices = lax.axis_size("seq")
    pairs = [(i, i + by) for i in range(devices) if 0 <= i + by < devices]
    return lax.ppermute(value, "seq", pairs)


def head_spread(value):
    devices = lax.axis_size("seq")
    came = 0
    for j in range(MP):
        pairs = [(s * MP, (s - 1) * MP + j) for s in range(1, devices)]
        came = came + lax.ppermute(value, ("seq", "mp"), pairs)
    return came


def dot(left, right, contract=((1,), (0,))):
    return lax.dot_general(left, right, (contract, ((), ())), preferred_element_type=FULL)


BY_ROWS = ((1,), (1,))
OVER_TOKENS = ((0,), (0,))


def send_rows(parts):
    return {o: lax.ppermute(parts[o], "mp", ring_shift(MP, o)) for o in (2, 1, 3)}


def gather_rows(rows, order=(2, 1, 3)):
    return {o: lax.ppermute(rows, "mp", ring_shift(MP, -o)) for o in order}


def take(value, index, axis):
    return lax.dynamic_index_in_dim(value, index, axis, keepdims=False)


def seq_place():
    me = lax.axis_index("seq")
    return me % 2, (me // 2) % X_DIM, me // (2 * X_DIM)


def line_sum(part, name):
    _, x, z = seq_place()
    mine = x if name == "x" else z
    total = take(part, mine, 0).astype(FULL)
    for o in (2, 1, 3):
        shift = seq_shift(0, o, 0) if name == "x" else seq_shift(o, 0, 0)
        came = lax.ppermute(take(part, (mine + o) % 4, 0).astype(LOW), "seq", shift)
        total = total + came.astype(FULL)
    return total


def all_sum(value):
    value = value + lax.ppermute(value, "seq", seq_shift(0, 0, 1))
    for dz, dx in ((0, 1), (1, 0)):
        shifts = [seq_shift(dz * o, dx * o, 0) for o in (2, 1, 3)]
        value = value + sum(lax.ppermute(value, "seq", shift) for shift in shifts)
    return value


def chip_line_scatter(part):
    groups = [
        [seq_index(z, x, core) for x in range(X_DIM) for core in range(2)] for z in range(Z_DIM)
    ]
    return lax.psum_scatter(
        part, "seq", scatter_dimension=0, axis_index_groups=groups, tiled=True
    )


def after(values, *others):
    return lax.optimization_barrier((values, others))[0]


def turn(value, by):
    rows = value.shape[0]
    return lax.dynamic_slice_in_dim(jnp.concatenate([value, value], 0), by, rows, 0)


def inv_rms(values):
    return lax.rsqrt(jnp.mean(values * values, axis=1, keepdims=True) + EPS)


def norm_back(grad_unit, unit_rows, inv_rows):
    return inv_rows * (
        grad_unit - unit_rows * jnp.mean(grad_unit * unit_rows, axis=1, keepdims=True)
    )


def whole(shape):
    return pl.BlockSpec(shape, lambda i, s, t: (0,) * len(shape))


def quarter(o, rows, width):
    return pl.BlockSpec((rows, width), lambda i, s, t: ((s[0] + o) % MP, 0))


def call(kernel, place, inputs, outs, grid=1, vmem=0, scratch=()):
    in_specs = [spec or whole(array.shape) for array, spec in inputs]
    out_specs = [spec or whole(shape) for shape, _, spec in outs]
    held = 0
    for (array, _), spec in zip(inputs, in_specs):
        held += math.prod(spec.block_shape) * array.dtype.itemsize
    for (_, dtype, _), spec in zip(outs, out_specs):
        held += math.prod(spec.block_shape) * jnp.dtype(dtype).itemsize
    return pl.pallas_call(
        kernel,
        grid_spec=pltpu.PrefetchScalarGridSpec(
            num_scalar_prefetch=2, grid=(grid,), in_specs=in_specs, out_specs=out_specs,
            scratch_shapes=scratch,
        ),
        out_shape=[jax.ShapeDtypeStruct(shape, dtype) for shape, dtype, _ in outs],
        compiler_params=pltpu.CompilerParams(vmem_limit_bytes=vmem or 2 * held + (8 << 20)),
        cost_estimate=pl.CostEstimate(flops=0, bytes_accessed=0, transcendentals=0),
    )(*place, *[array for array, _ in inputs])


def places(s_ref, rows, columns):
    row = lax.broadcasted_iota(jnp.int32, (rows, columns), 0) + s_ref[0] * (rows // MP)
    return jnp.where(row >= rows, row - rows, row)


def taps(s_ref, t_ref, mixed, tail_mixed):
    rows, columns = mixed.shape
    place = places(s_ref, rows, columns)
    keep_one = place != t_ref[0]
    keep_two = keep_one & (place != t_ref[0] + 1)
    back_one = pltpu.roll(mixed, 1, 0)
    back_two = pltpu.roll(mixed, 2, 0)
    last = tail_mixed[7:8]
    before_last = tail_mixed[6:7]
    tap_one = jnp.where(keep_one, jnp.where(place == 0, last, back_one), 0.0)
    tap_two = jnp.where(
        keep_two, jnp.where(place == 0, before_last, jnp.where(place == 1, last, back_two)), 0.0
    )
    return place, keep_one, keep_two, tap_one, tap_two


def mix_kernel(
    s_ref, t_ref, h0_ref, h1_ref, h2_ref, h3_ref, tail_ref, gain_ref, w_ref, conv_ref, out_ref,
    normed_ref, b_ref, c_ref, x_ref,
    gated_ref, convolved_ref, tail_mixed_ref, p0_ref, p1_ref, p2_ref, p3_ref,
):
    gain = gain_ref[...]
    rows = p0_ref.shape[0]
    for o, ref in enumerate((h0_ref, h1_ref, h2_ref, h3_ref)):
        hidden = ref[...]
        normed_ref[o * rows : (o + 1) * rows, :] = (hidden * inv_rms(hidden) * gain).astype(LOW)
    normed = normed_ref[...]
    parts = [dot(normed, w_ref[k]) for k in range(3)]
    for part, ref in zip(parts, (b_ref, c_ref, x_ref)):
        ref[...] = part
    tail = tail_ref[...]
    tail = (tail * inv_rms(tail) * gain).astype(LOW)
    tail_mixed = (dot(tail, w_ref[0]) * dot(tail, w_ref[2])).astype(LOW).astype(FULL)
    tail_mixed_ref[...] = tail_mixed
    mixed = (parts[0] * parts[2]).astype(LOW).astype(FULL)
    _, _, _, tap_one, tap_two = taps(s_ref, t_ref, mixed, tail_mixed)
    conv = conv_ref[...]
    convolved = conv[0:1] * tap_two + conv[1:2] * tap_one + conv[2:3] * mixed
    convolved_ref[...] = convolved
    gated = (parts[1] * convolved).astype(LOW)
    gated_ref[...] = gated
    branch = dot(gated, out_ref[...])
    for o, ref in enumerate((p0_ref, p1_ref, p2_ref, p3_ref)):
        ref[...] = branch[o * rows : (o + 1) * rows].astype(ref.dtype)


def middle_kernel(s_ref, t_ref, hidden_ref, p0_ref, r1_ref, r2_ref, r3_ref, middle_ref, low_ref):
    total = hidden_ref[...] + p0_ref[...]
    for ref in (r1_ref, r2_ref, r3_ref):
        total = total + ref[...].astype(FULL)
    middle_ref[...] = total
    low_ref[...] = total.astype(LOW)


def slabs_of(part, order):
    return jnp.concatenate([part[i * 32 : (i + 1) * 32] for i in order], 0)


BIG = 60 << 20
SCATTER_ORDER = [
    seq_index(z, x, core) for x in range(X_DIM) for core in range(2) for z in range(Z_DIM)
]


def ffn_grad_kernel(
    steps, s_ref, t_ref, normed_ref, grad_gu_ref, low_ref, active_ref, part_ref, turned_ref
):
    step = pl.program_id(0)

    @pl.when(step == 0)
    def _():
        turned_ref[...] = jnp.transpose(normed_ref[...])

    @pl.when(step == steps)
    def _():
        turned_ref[...] = jnp.transpose(low_ref[...])

    @pl.when(step < steps)
    def _():
        part_ref[...] = slabs_of(dot(turned_ref[...], grad_gu_ref[...]).astype(LOW), SCATTER_ORDER)

    @pl.when(step >= steps)
    def _():
        part_ref[...] = slabs_of(dot(turned_ref[...], active_ref[...]).astype(LOW), SCATTER_ORDER)


def ffn_out_kernel(s_ref, t_ref, active_ref, down_ref, out_ref):
    part = dot(active_ref[...], down_ref[...]).astype(LOW)
    rows = part.shape[0] // MP
    for i, o in enumerate(ORDER):
        place = lax.rem(s_ref[0] + o, MP) * rows
        out_ref[pl.ds(pl.multiple_of(place, rows), rows), :] = part[i * rows : (i + 1) * rows]


def place_kernel(s_ref, t_ref, c0_ref, c1_ref, c2_ref, c3_ref, out_ref):
    for o, ref in enumerate((c0_ref, c1_ref, c2_ref, c3_ref)):

        @pl.when(pl.program_id(0) == o)
        def _():
            out_ref[...] = ref[...].astype(FULL)


def place_add_kernel(s_ref, t_ref, c0_ref, c1_ref, c2_ref, c3_ref, more_ref, out_ref):
    for o, ref in enumerate((c0_ref, c1_ref, c2_ref, c3_ref)):

        @pl.when(pl.program_id(0) == o)
        def _():
            out_ref[...] = ref[...].astype(FULL) + more_ref[...].astype(FULL)


def branch_kernel(
    s_ref, t_ref, p0_ref, r1_ref, r2_ref, r3_ref, middle_ref, gain_ref, out_grad_ref,
    grad_ref, low_ref, gain_part_ref,
):
    total = p0_ref[...].astype(FULL)
    for ref in (r1_ref, r2_ref, r3_ref):
        total = total + ref[...].astype(FULL)
    middle = middle_ref[...]
    inv = inv_rms(middle)
    unit = middle * inv
    gain_part_ref[...] = jnp.sum(total * unit, axis=0, keepdims=True)
    grad = out_grad_ref[...] + norm_back(total * gain_ref[...], unit, inv)
    grad_ref[...] = grad
    low_ref[...] = grad.astype(LOW)


def mix_back_kernel(
    s_ref, t_ref, g0_ref, g1_ref, g2_ref, g3_ref, gated_ref, head_ref, head_c_ref, b_ref, c_ref, x_ref,
    convolved_ref, tail_mixed_ref, conv_ref, out_ref, w_ref, normed_ref, gain_ref,
    ffn_gain_ref, part_ref, conv_part_ref, p0_ref, p1_ref, p2_ref, p3_ref,
):
    out_weight = out_ref[...]
    conv = conv_ref[...]
    grad_gated = jnp.concatenate(
        [dot(ref[...], out_weight, BY_ROWS) for ref in (g0_ref, g1_ref, g2_ref, g3_ref)], 0
    )
    head = dot(head_ref[...], out_weight, BY_ROWS)[:8] * head_c_ref[...]
    came_before_last = conv[0:1] * head[0:1]
    came_last = conv[0:1] * head[1:2] + conv[1:2] * head[0:1]
    b_part, c_part, x_part = b_ref[...], c_ref[...], x_ref[...]
    mixed = (b_part * x_part).astype(LOW).astype(FULL)
    place, keep_one, keep_two, tap_one, tap_two = taps(s_ref, t_ref, mixed, tail_mixed_ref[...])
    rows = mixed.shape[0]
    grad_conv = grad_gated * c_part
    conv_part_ref[...] = jnp.concatenate(
        [jnp.sum(grad_conv * tap, axis=0, keepdims=True) for tap in (tap_two, tap_one, mixed)], 0
    )
    to_one = jnp.where(keep_one, conv[1:2] * grad_conv, 0.0)
    to_two = jnp.where(keep_two, conv[0:1] * grad_conv, 0.0)
    from_one = pltpu.roll(to_one, rows - 1, 0)
    from_two = pltpu.roll(to_two, rows - 2, 0)
    is_last, is_before_last = place == rows - 1, place == rows - 2
    grad_mixed = (
        conv[2:3] * grad_conv
        + jnp.where(is_last, came_last, from_one)
        + jnp.where(is_last, 0.0, jnp.where(is_before_last, came_before_last, from_two))
    )
    grad_mixed = grad_mixed.astype(LOW).astype(FULL)
    grads = [
        (grad_mixed * x_part).astype(LOW),
        (grad_gated * convolved_ref[...]).astype(LOW),
        (grad_mixed * b_part).astype(LOW),
    ]
    columns = mixed.shape[1]
    turned = jnp.transpose(normed_ref[...])
    for k, grad in enumerate(grads):
        part_ref[:, k * columns : (k + 1) * columns] = slabs_of(
            dot(turned, grad).astype(LOW), SCATTER_ORDER
        )
    branch = jnp.concatenate([ref[...] for ref in (g0_ref, g1_ref, g2_ref, g3_ref)], 0)
    part_ref[:, 3 * columns :] = slabs_of(
        dot(jnp.transpose(branch), gated_ref[...]).astype(LOW), SCATTER_ORDER
    )
    quarter_rows = rows // MP
    sends = (p0_ref, p1_ref, p2_ref, p3_ref)
    gain_part = 0.0
    for o, ref in enumerate(sends):
        cut = slice(o * quarter_rows, (o + 1) * quarter_rows)
        part = sum(dot(grads[k][cut], w_ref[k], BY_ROWS) for k in range(3))
        ref[:quarter_rows, :] = part.astype(ref.dtype)
        gain_part = gain_part + jnp.sum(
            part * normed_ref[cut, :].astype(FULL), axis=0, keepdims=True
        )
    spare = jnp.zeros((14, gain_part.shape[1]), FULL)
    small = jnp.concatenate([gain_part / gain_ref[...], ffn_gain_ref[...], spare], 0)
    for ref in sends:
        ref[quarter_rows:, :] = small.astype(ref.dtype)


def hidden_kernel(
    s_ref, t_ref, p0_ref, r1_ref, r2_ref, r3_ref, hidden_ref, gain_ref, grad_ref,
    low_ref, small_ref,
):
    total = p0_ref[...]
    for ref in (r1_ref, r2_ref, r3_ref):
        total = total + ref[...].astype(FULL)
    rows = hidden_ref.shape[0]
    small_ref[...] = total[rows:]
    hidden = hidden_ref[...]
    inv = inv_rms(hidden)
    grad = grad_ref[...] + norm_back(total[:rows] * gain_ref[...], hidden * inv, inv)
    low_ref[...] = grad.astype(LOW)


def on_device(
    hidden_in,
    mix_gain,
    in_weight,
    conv_weight,
    out_weight,
    ffn_gain,
    gate_up_weight,
    down_weight,
    seq_starts,
    out_grad,
):
    rows, width = hidden_in.shape
    mine = rows // MP
    channels = conv_weight.shape[1]
    hidden_units = down_weight.shape[0]
    me = lax.axis_index("mp")
    start = me * mine
    natural = (rows - start) % rows
    place = (me.astype(jnp.int32)[None], seq_starts)
    mix_gain = mix_gain[None]
    ffn_gain = ffn_gain[None]
    w_in = jnp.transpose(in_weight, (1, 0, 2))
    w_gu = jnp.transpose(gate_up_weight, (1, 0, 2))
    own_rows = quarter(0, mine, width)

    tail_in = slab_shift(hidden_in[rows - 8 :], 1)
    quarter_low = ((mine, width), LOW, None)
    quarter_full = ((mine, width), FULL, None)
    low_part = ((rows, channels), LOW, None)
    full_part = ((rows, channels), FULL, None)
    outs = call(
        mix_kernel,
        place,
        [(hidden_in, quarter(o, mine, width)) for o in range(MP)]
        + [(v, None) for v in (tail_in, mix_gain, w_in, conv_weight, out_weight)],
        [((rows, width), LOW, None), full_part, full_part, full_part]
        + [low_part, full_part, ((8, channels), FULL, None)]
        + [quarter_full, quarter_low, quarter_low, quarter_low],
        vmem=BIG,
    )
    normed, b_part, c_part, x_part, gated, convolved, tail_mixed, p0, p1, p2, p3 = outs
    came = send_rows({1: p1, 2: p2, 3: p3})
    w_gu = after(gate_up_weight, came[1]).reshape(width, -1)
    came, w_gu = lax.optimization_barrier((came, w_gu))
    middle, middle_low = call(
        middle_kernel,
        place,
        [(hidden_in, own_rows), (p0, None), (came[1], None), (came[2], None), (came[3], None)],
        [quarter_full, quarter_low],
    )
    mids = {0: middle_low, **gather_rows(middle_low, (1, 3, 2))}
    late_grad = after(out_grad, middle_low)
    grad_low = jnp.concatenate(
        [lax.dynamic_slice_in_dim(late_grad, ((me + o) % MP) * mine, mine, 0) for o in ORDER], 0
    ).astype(LOW)
    grad_active = dot(grad_low, down_weight, BY_ROWS)
    mids[1], mids[3], grad_active = lax.optimization_barrier((mids[1], mids[3], grad_active))

    def ffn(offsets, grad_active):
        middle = jnp.concatenate([mids[o] for o in offsets], 0).astype(FULL)
        normed = (middle * inv_rms(middle) * ffn_gain).astype(LOW)
        gate_up = dot(normed, w_gu)
        gate, upper = gate_up[:, :hidden_units], gate_up[:, hidden_units:]
        sigma = jax.nn.sigmoid(gate)
        active = (gate * sigma * upper).astype(LOW)
        grad_gate = grad_active * upper * sigma * (1.0 + gate * (1.0 - sigma))
        grad_upper = grad_active * gate * sigma
        grad_gu = jnp.concatenate([grad_gate.astype(LOW), grad_upper.astype(LOW)], 1)
        back = dot(grad_gu, w_gu, BY_ROWS)
        return normed, active, grad_gu, back

    near = ffn(ORDER[:3], grad_active[: 3 * mine])
    near_low = near[3].astype(LOW)
    p0 = near_low[:mine]
    came_near = [
        lax.ppermute(near_low[mine : 2 * mine], "mp", ring_shift(MP, 1)),
        lax.ppermute(near_low[2 * mine :], "mp", ring_shift(MP, 3)),
    ]
    mids[2], far_grad = after((mids[2], grad_active[3 * mine :]), near_low)
    far = ffn(ORDER[3:], far_grad)
    far_low = far[3].astype(LOW)
    came = [*came_near, lax.ppermute(far_low, "mp", ring_shift(MP, 2))]
    normed_two, active, grad_gu = [
        jnp.concatenate([a, b], 0) for a, b in zip(near[:3], far[:3])
    ]
    normed_two, active, grad_gu, grad_low = after(
        (normed_two, active, grad_gu, grad_low), far_low
    )
    ffn_part = call(
        ffn_out_kernel,
        place,
        [(active, None), (down_weight, None)],
        [((rows, width), LOW, None)],
        vmem=BIG,
    )[0]
    ffn_out = lax.psum(ffn_part, "mp")
    normed_two, active, grad_gu, grad_low = after(
        (normed_two, active, grad_gu, grad_low), came_near[0]
    )
    block = hidden_units
    steps = 2 * hidden_units // block
    gate_up_block = pl.BlockSpec((rows, block), lambda i, s, t: (0, jnp.minimum(i, steps - 1)))
    down_block = pl.BlockSpec((rows, block), lambda i, s, t: (0, jnp.maximum(i - steps, 0)))
    ffn_grad_part = call(
        functools.partial(ffn_grad_kernel, steps),
        place,
        [(normed_two, None), (grad_gu, gate_up_block), (grad_low, None), (active, down_block)],
        [
            (
                (width, 3 * hidden_units),
                LOW,
                pl.BlockSpec((width, block), lambda i, s, t: (0, i)),
            )
        ],
        grid=3 * hidden_units // block,
        scratch=[pltpu.VMEM((width, rows), LOW)],
        vmem=BIG,
    )[0]
    ffn_line = chip_line_scatter(ffn_grad_part)
    head_c = lax.dynamic_slice_in_dim(after(c_part, near_low), natural, 8, 0)
    head_c = slab_shift(head_c, -1)
    came, ffn_part, head_c, ffn_grad_part = lax.optimization_barrier(
        (tuple(came), ffn_part, head_c, ffn_grad_part)
    )
    grad_middle, grad_branch, ffn_gain_part = call(
        branch_kernel,
        place,
        [(v, None) for v in (p0, *came, middle, ffn_gain)] + [(out_grad, own_rows)],
        [quarter_full, quarter_low, ((1, width), FULL, None)],
        vmem=BIG,
    )
    branches = {o: lax.ppermute(grad_branch, "mp", ring_shift(MP, -o)) for o in (1, 3)}
    head = head_spread(grad_branch[:16])
    branches[2] = lax.ppermute(after(grad_branch, head), "mp", ring_shift(MP, 2))
    branches, head = lax.optimization_barrier((branches, head))

    outs = call(
        mix_back_kernel,
        place,
        [(grad_branch, None)]
        + [(branches[o], None) for o in (1, 2, 3)]
        + [
            (v, None)
            for v in (
                gated, head, head_c, b_part, c_part, x_part, convolved, tail_mixed, conv_weight,
                out_weight, w_in, normed, mix_gain, ffn_gain_part,
            )
        ],
        [((width, 4 * channels), LOW, None), ((3, channels), FULL, None)]
        + [((mine + 16, width), LOW if o else FULL, None) for o in range(MP)],
        vmem=BIG,
    )
    in_out_part, conv_part, p0, p1, p2, p3 = outs
    in_out_line = chip_line_scatter(in_out_part)
    came = send_rows({1: p1, 2: p2, 3: p3})
    hidden_low, small = call(
        hidden_kernel,
        place,
        [(v, None) for v in (p0, came[1], came[2], came[3])]
        + [(hidden_in, own_rows), (mix_gain, None), (grad_middle, None)],
        [quarter_low, ((16, width), FULL, None)],
    )
    ends = gather_rows(hidden_low)
    conv_row = jnp.pad(conv_part.reshape(1, -1), ((0, 0), (0, width - 3 * channels)))
    small = all_sum(jnp.concatenate([small[:2], conv_row], 0))
    ends, ffn_out, ffn_line = lax.optimization_barrier((ends, ffn_out, ffn_line))
    chunk = pl.BlockSpec((mine, width), lambda i, s, t: ((s[0] + i) % MP, 0))
    hidden_grad = call(
        place_kernel,
        place,
        [(v, None) for v in (hidden_low, ends[1], ends[2], ends[3])],
        [((rows, width), FULL, chunk)],
        grid=MP,
    )[0]
    hidden_out = call(
        place_add_kernel,
        place,
        [(mids[o], None) for o in range(MP)] + [(ffn_out, chunk)],
        [((rows, width), FULL, chunk)],
        grid=MP,
    )[0]
    in_out_line, small = after((in_out_line, small), hidden_grad, hidden_out)
    line = jnp.concatenate([ffn_line, in_out_line], 1).reshape(Z_DIM, 32, -1)
    done = line_sum(line, "z")
    ffn_done = done[:, : 3 * hidden_units]
    in_out_done = done[:, 3 * hidden_units :]
    mix_gain_grad, ffn_gain_grad = small[0], small[1]
    conv_weight_grad = small[2, : 3 * channels].reshape(3, channels)
    local = in_out_done.shape[0]
    return (
        hidden_out,
        hidden_grad,
        mix_gain_grad,
        in_out_done[:, : 3 * channels].reshape(local, 3, channels),
        conv_weight_grad,
        in_out_done[:, 3 * channels :].T,
        ffn_gain_grad,
        ffn_done[:, : 2 * hidden_units].reshape(local, 2, hidden_units),
        ffn_done[:, 2 * hidden_units :].T,
    )


def solution(mesh):
    placed = (
        P("seq", None),
        P(),
        P(None, None, "mp"),
        P(None, "mp"),
        P("mp", None),
        P(),
        P(None, None, "mp"),
        P("mp", None),
        P("seq"),
        P("seq", None),
    )
    return jax.shard_map(
        on_device,
        mesh=mesh,
        in_specs=placed,
        out_specs=(
            P("seq", None),
            P("seq", None),
            P(),
            P("seq", None, "mp"),
            P(None, "mp"),
            P("mp", "seq"),
            P(),
            P("seq", None, "mp"),
            P("mp", "seq"),
        ),
        check_vma=False,
    )
```

```python
import functools
import math

import jax
import jax.numpy as jnp
from jax import lax
from jax.experimental import pallas as pl
from jax.experimental.pallas import tpu as pltpu
from jax.sharding import PartitionSpec as P

EPS = 1e-05
LOW = jnp.bfloat16
FULL = jnp.float32
MP = 4
X_DIM = 4
LANES = 128
ORDER = (0, 1, 3, 2)
Z_DIM = 4


def ring_shift(size, by):
    return [(i, (i + by) % size) for i in range(size)]


def seq_index(z, x, core):
    return (z * X_DIM + x) * 2 + core


def seq_shift(dz, dx, flip):
    return [
        (
            seq_index(z, x, core),
            seq_index((z + dz) % Z_DIM, (x + dx) % X_DIM, core ^ flip),
        )
        for z in range(Z_DIM)
        for x in range(X_DIM)
        for core in range(2)
    ]


def slab_shift(value, by):
    devices = lax.axis_size("seq")
    pairs = [(i, i + by) for i in range(devices) if 0 <= i + by < devices]
    return lax.ppermute(value, "seq", pairs)


def head_spread(value):
    devices = lax.axis_size("seq")
    came = 0
    for j in range(MP):
        pairs = [(s * MP, (s - 1) * MP + j) for s in range(1, devices)]
        came = came + lax.ppermute(value, ("seq", "mp"), pairs)
    return came


def dot(left, right, contract=((1,), (0,))):
    return lax.dot_general(left, right, (contract, ((), ())), preferred_element_type=FULL)


BY_ROWS = ((1,), (1,))
OVER_TOKENS = ((0,), (0,))


def send_rows(parts):
    return {o: lax.ppermute(parts[o], "mp", ring_shift(MP, o)) for o in (2, 1, 3)}


def gather_rows(rows, order=(2, 1, 3)):
    return {o: lax.ppermute(rows, "mp", ring_shift(MP, -o)) for o in order}


def take(value, index, axis):
    return lax.dynamic_index_in_dim(value, index, axis, keepdims=False)


def seq_place():
    me = lax.axis_index("seq")
    return me % 2, (me // 2) % X_DIM, me // (2 * X_DIM)


def chip_line_scatter(part):
    groups = [
        [seq_index(z, x, core) for x in range(X_DIM) for core in range(2)] for z in range(Z_DIM)
    ]
    return lax.psum_scatter(
        part, "seq", scatter_dimension=0, axis_index_groups=groups, tiled=True
    )


def after(values, *others):
    return lax.optimization_barrier((values, others))[0]


def turn(value, by):
    rows = value.shape[0]
    return lax.dynamic_slice_in_dim(jnp.concatenate([value, value], 0), by, rows, 0)


def inv_rms(values):
    return lax.rsqrt(jnp.mean(values * values, axis=1, keepdims=True) + EPS)


def norm_back(grad_unit, unit_rows, inv_rows):
    return inv_rows * (
        grad_unit - unit_rows * jnp.mean(grad_unit * unit_rows, axis=1, keepdims=True)
    )


def whole(shape):
    return pl.BlockSpec(shape, lambda i, s, t: (0,) * len(shape))


def quarter(o, rows, width):
    return pl.BlockSpec((rows, width), lambda i, s, t: ((s[0] + o) % MP, 0))


def call(kernel, place, inputs, outs, grid=1, vmem=0, scratch=(), flops=0):
    in_specs = [spec or whole(array.shape) for array, spec in inputs]
    out_specs = [spec or whole(shape) for shape, _, spec in outs]
    held = 0
    for (array, _), spec in zip(inputs, in_specs):
        held += math.prod(spec.block_shape) * array.dtype.itemsize
    for (_, dtype, _), spec in zip(outs, out_specs):
        held += math.prod(spec.block_shape) * jnp.dtype(dtype).itemsize
    return pl.pallas_call(
        kernel,
        grid_spec=pltpu.PrefetchScalarGridSpec(
            num_scalar_prefetch=2, grid=(grid,), in_specs=in_specs, out_specs=out_specs,
            scratch_shapes=scratch,
        ),
        out_shape=[jax.ShapeDtypeStruct(shape, dtype) for shape, dtype, _ in outs],
        compiler_params=pltpu.CompilerParams(vmem_limit_bytes=vmem or 2 * held + (8 << 20)),
        cost_estimate=pl.CostEstimate(flops=flops, bytes_accessed=0, transcendentals=0),
    )(*place, *[array for array, _ in inputs])


def places(s_ref, rows, columns):
    row = lax.broadcasted_iota(jnp.int32, (rows, columns), 0) + s_ref[0] * (rows // MP)
    return jnp.where(row >= rows, row - rows, row)


def taps(s_ref, t_ref, mixed, tail_mixed):
    rows, columns = mixed.shape
    place = places(s_ref, rows, columns)
    keep_one = place != t_ref[0]
    keep_two = keep_one & (place != t_ref[0] + 1)
    back_one = pltpu.roll(mixed, 1, 0)
    back_two = pltpu.roll(mixed, 2, 0)
    last = tail_mixed[7:8]
    before_last = tail_mixed[6:7]
    tap_one = jnp.where(keep_one, jnp.where(place == 0, last, back_one), 0.0)
    tap_two = jnp.where(
        keep_two, jnp.where(place == 0, before_last, jnp.where(place == 1, last, back_two)), 0.0
    )
    return place, keep_one, keep_two, tap_one, tap_two


def mix_kernel(
    s_ref, t_ref, h0_ref, h1_ref, h2_ref, h3_ref, tail_ref, gain_ref, w_ref, conv_ref, out_ref,
    normed_ref, b_ref, c_ref, x_ref,
    gated_ref, convolved_ref, tail_mixed_ref, p0_ref, p1_ref, p2_ref, p3_ref,
):
    gain = gain_ref[...]
    rows = p0_ref.shape[0]
    for o, ref in enumerate((h0_ref, h1_ref, h2_ref, h3_ref)):
        hidden = ref[...]
        normed_ref[o * rows : (o + 1) * rows, :] = (hidden * inv_rms(hidden) * gain).astype(LOW)
    normed = normed_ref[...]
    parts = [dot(normed, w_ref[k]) for k in range(3)]
    for part, ref in zip(parts, (b_ref, c_ref, x_ref)):
        ref[...] = part
    tail = tail_ref[...]
    tail = (tail * inv_rms(tail) * gain).astype(LOW)
    tail_mixed = (dot(tail, w_ref[0]) * dot(tail, w_ref[2])).astype(LOW).astype(FULL)
    tail_mixed_ref[...] = tail_mixed
    mixed = (parts[0] * parts[2]).astype(LOW).astype(FULL)
    _, _, _, tap_one, tap_two = taps(s_ref, t_ref, mixed, tail_mixed)
    conv = conv_ref[...]
    convolved = conv[0:1] * tap_two + conv[1:2] * tap_one + conv[2:3] * mixed
    convolved_ref[...] = convolved
    gated = (parts[1] * convolved).astype(LOW)
    gated_ref[...] = gated
    branch = dot(gated, out_ref[...])
    for o, ref in enumerate((p0_ref, p1_ref, p2_ref, p3_ref)):
        ref[...] = branch[o * rows : (o + 1) * rows].astype(ref.dtype)


def middle_kernel(s_ref, t_ref, hidden_ref, p0_ref, r1_ref, r2_ref, r3_ref, middle_ref, low_ref):
    total = hidden_ref[...] + p0_ref[...]
    for ref in (r1_ref, r2_ref, r3_ref):
        total = total + ref[...].astype(FULL)
    middle_ref[...] = total
    low_ref[...] = total.astype(LOW)


def slabs_of(part, order):
    return jnp.concatenate([part[i * 32 : (i + 1) * 32] for i in order], 0)


BIG = 60 << 20
SCATTER_ORDER = [
    seq_index(z, x, core) for x in range(X_DIM) for core in range(2) for z in range(Z_DIM)
]


def ffn_grad_kernel(
    steps, s_ref, t_ref, normed_ref, grad_gu_ref, low_ref, active_ref, part_ref, turned_ref
):
    step = pl.program_id(0)

    @pl.when(step == 0)
    def _():
        turned_ref[...] = jnp.transpose(normed_ref[...])

    @pl.when(step == steps)
    def _():
        turned_ref[...] = jnp.transpose(low_ref[...])

    @pl.when(step < steps)
    def _():
        part_ref[...] = slabs_of(dot(turned_ref[...], grad_gu_ref[...]).astype(LOW), SCATTER_ORDER)

    @pl.when(step >= steps)
    def _():
        part_ref[...] = slabs_of(dot(turned_ref[...], active_ref[...]).astype(LOW), SCATTER_ORDER)


def ffn_out_kernel(s_ref, t_ref, active_ref, down_ref, out_ref):
    part = dot(active_ref[...], down_ref[...]).astype(LOW)
    rows = part.shape[0] // MP
    for i, o in enumerate(ORDER):
        place = lax.rem(s_ref[0] + o, MP) * rows
        out_ref[pl.ds(pl.multiple_of(place, rows), rows), :] = part[i * rows : (i + 1) * rows]


def place_kernel(s_ref, t_ref, c0_ref, c1_ref, c2_ref, c3_ref, out_ref):
    for o, ref in enumerate((c0_ref, c1_ref, c2_ref, c3_ref)):

        @pl.when(pl.program_id(0) == o)
        def _():
            out_ref[...] = ref[...].astype(FULL)


def place_add_kernel(s_ref, t_ref, c0_ref, c1_ref, c2_ref, c3_ref, more_ref, out_ref):
    for o, ref in enumerate((c0_ref, c1_ref, c2_ref, c3_ref)):

        @pl.when(pl.program_id(0) == o)
        def _():
            out_ref[...] = ref[...].astype(FULL) + more_ref[...].astype(FULL)


def branch_kernel(
    s_ref, t_ref, p0_ref, r1_ref, r2_ref, r3_ref, middle_ref, gain_ref, out_grad_ref,
    grad_ref, low_ref, gain_part_ref,
):
    total = p0_ref[...].astype(FULL)
    for ref in (r1_ref, r2_ref, r3_ref):
        total = total + ref[...].astype(FULL)
    middle = middle_ref[...]
    inv = inv_rms(middle)
    unit = middle * inv
    gain_part_ref[...] = jnp.sum(total * unit, axis=0, keepdims=True)
    grad = out_grad_ref[...] + norm_back(total * gain_ref[...], unit, inv)
    grad_ref[...] = grad
    low_ref[...] = grad.astype(LOW)


def mix_back_kernel(
    s_ref, t_ref, g0_ref, g1_ref, g2_ref, g3_ref, gated_ref, head_ref, head_c_ref, b_ref, c_ref, x_ref,
    convolved_ref, tail_mixed_ref, conv_ref, out_ref, w_ref, normed_ref, gain_ref,
    ffn_gain_ref, part_ref, p0_ref, p1_ref, p2_ref, p3_ref,
):
    out_weight = out_ref[...]
    conv = conv_ref[...]
    grad_gated = jnp.concatenate(
        [dot(ref[...], out_weight, BY_ROWS) for ref in (g0_ref, g1_ref, g2_ref, g3_ref)], 0
    )
    head = dot(head_ref[...], out_weight, BY_ROWS)[:8] * head_c_ref[...]
    came_before_last = conv[0:1] * head[0:1]
    came_last = conv[0:1] * head[1:2] + conv[1:2] * head[0:1]
    b_part, c_part, x_part = b_ref[...], c_ref[...], x_ref[...]
    mixed = (b_part * x_part).astype(LOW).astype(FULL)
    place, keep_one, keep_two, tap_one, tap_two = taps(s_ref, t_ref, mixed, tail_mixed_ref[...])
    rows = mixed.shape[0]
    grad_conv = grad_gated * c_part
    conv_part = [
        jnp.sum(grad_conv * tap, axis=0, keepdims=True) for tap in (tap_two, tap_one, mixed)
    ]
    to_one = jnp.where(keep_one, conv[1:2] * grad_conv, 0.0)
    to_two = jnp.where(keep_two, conv[0:1] * grad_conv, 0.0)
    from_one = pltpu.roll(to_one, rows - 1, 0)
    from_two = pltpu.roll(to_two, rows - 2, 0)
    is_last, is_before_last = place == rows - 1, place == rows - 2
    grad_mixed = (
        conv[2:3] * grad_conv
        + jnp.where(is_last, came_last, from_one)
        + jnp.where(is_last, 0.0, jnp.where(is_before_last, came_before_last, from_two))
    )
    grad_mixed = grad_mixed.astype(LOW).astype(FULL)
    grads = [
        (grad_mixed * x_part).astype(LOW),
        (grad_gated * convolved_ref[...]).astype(LOW),
        (grad_mixed * b_part).astype(LOW),
    ]
    columns = mixed.shape[1]
    turned = jnp.transpose(normed_ref[...])
    for k, grad in enumerate(grads):
        part_ref[:, k * columns : (k + 1) * columns] = slabs_of(
            dot(turned, grad).astype(LOW), SCATTER_ORDER
        )
    branch = jnp.concatenate([ref[...] for ref in (g0_ref, g1_ref, g2_ref, g3_ref)], 0)
    part_ref[:, 3 * columns : 4 * columns] = slabs_of(
        dot(jnp.transpose(branch), gated_ref[...]).astype(LOW), SCATTER_ORDER
    )
    quarter_rows = rows // MP
    sends = (p0_ref, p1_ref, p2_ref, p3_ref)
    gain_part = 0.0
    for o, ref in enumerate(sends):
        cut = slice(o * quarter_rows, (o + 1) * quarter_rows)
        part = sum(dot(grads[k][cut], w_ref[k], BY_ROWS) for k in range(3))
        ref[...] = part.astype(ref.dtype)
        gain_part = gain_part + jnp.sum(
            part * normed_ref[cut, :].astype(FULL), axis=0, keepdims=True
        )
    conv_row = jnp.concatenate([*conv_part, jnp.zeros_like(conv_part[0])], 1)
    small = [gain_part / gain_ref[...], ffn_gain_ref[...], conv_row]
    lanes = part_ref.shape[1] - 4 * columns
    pieces = [row[:, i : i + lanes] for row in small for i in range(0, row.shape[1], lanes)]
    tile = jnp.concatenate([*pieces, jnp.zeros((8, lanes), FULL)], 0).astype(LOW)
    part_ref[:, 4 * columns :] = jnp.concatenate([tile] * (part_ref.shape[0] // 32), 0)


def hidden_kernel(
    s_ref, t_ref, p0_ref, r1_ref, r2_ref, r3_ref, hidden_ref, gain_ref, grad_ref, low_ref
):
    total = p0_ref[...]
    for ref in (r1_ref, r2_ref, r3_ref):
        total = total + ref[...].astype(FULL)
    hidden = hidden_ref[...]
    inv = inv_rms(hidden)
    grad = grad_ref[...] + norm_back(total * gain_ref[...], hidden * inv, inv)
    low_ref[...] = grad.astype(LOW)


def finish_kernel(s_ref, t_ref, *refs):
    in_ref, out_ref, gate_up_ref, down_ref, small_ref = refs[8:]

    def total(parts, start, size):
        return sum(ref[:, start : start + size].astype(FULL) for ref in parts)

    ffn_parts, mix_parts = refs[:4], refs[4:8]
    units = down_ref.shape[1]
    channels = out_ref.shape[1]
    for k in range(2):
        gate_up_ref[k] = total(ffn_parts, k * units, units)
    down_ref[...] = total(ffn_parts, 2 * units, units)
    for k in range(3):
        in_ref[k] = total(mix_parts, k * channels, channels)
    out_ref[...] = total(mix_parts, 3 * channels, channels)
    small_ref[...] = total(mix_parts, 4 * channels, LANES)


def on_device(
    hidden_in,
    mix_gain,
    in_weight,
    conv_weight,
    out_weight,
    ffn_gain,
    gate_up_weight,
    down_weight,
    seq_starts,
    out_grad,
):
    rows, width = hidden_in.shape
    mine = rows // MP
    channels = conv_weight.shape[1]
    hidden_units = down_weight.shape[0]
    me = lax.axis_index("mp")
    start = me * mine
    natural = (rows - start) % rows
    place = (me.astype(jnp.int32)[None], seq_starts)
    mix_gain = mix_gain[None]
    ffn_gain = ffn_gain[None]
    w_in = jnp.transpose(in_weight, (1, 0, 2))
    w_gu = jnp.transpose(gate_up_weight, (1, 0, 2))
    own_rows = quarter(0, mine, width)

    tail_in = slab_shift(hidden_in[rows - 8 :], 1)
    quarter_low = ((mine, width), LOW, None)
    quarter_full = ((mine, width), FULL, None)
    low_part = ((rows, channels), LOW, None)
    full_part = ((rows, channels), FULL, None)
    outs = call(
        mix_kernel,
        place,
        [(hidden_in, quarter(o, mine, width)) for o in range(MP)]
        + [(v, None) for v in (tail_in, mix_gain, w_in, conv_weight, out_weight)],
        [((rows, width), LOW, None), full_part, full_part, full_part]
        + [low_part, full_part, ((8, channels), FULL, None)]
        + [quarter_full, quarter_low, quarter_low, quarter_low],
        vmem=BIG,
    )
    normed, b_part, c_part, x_part, gated, convolved, tail_mixed, p0, p1, p2, p3 = outs
    came = send_rows({1: p1, 2: p2, 3: p3})
    w_gu = after(gate_up_weight, came[1]).reshape(width, -1)
    came, w_gu = lax.optimization_barrier((came, w_gu))
    middle, middle_low = call(
        middle_kernel,
        place,
        [(hidden_in, own_rows), (p0, None), (came[1], None), (came[2], None), (came[3], None)],
        [quarter_full, quarter_low],
    )
    mids = {0: middle_low, **gather_rows(middle_low, (1, 3, 2))}
    late_grad = after(out_grad, middle_low)
    grad_low = jnp.concatenate(
        [lax.dynamic_slice_in_dim(late_grad, ((me + o) % MP) * mine, mine, 0) for o in ORDER], 0
    ).astype(LOW)
    grad_active = dot(grad_low, down_weight, BY_ROWS)
    mids[1], mids[3], grad_active = lax.optimization_barrier((mids[1], mids[3], grad_active))

    def ffn(offsets, grad_active):
        middle = jnp.concatenate([mids[o] for o in offsets], 0).astype(FULL)
        normed = (middle * inv_rms(middle) * ffn_gain).astype(LOW)
        gate_up = dot(normed, w_gu)
        gate, upper = gate_up[:, :hidden_units], gate_up[:, hidden_units:]
        sigma = jax.nn.sigmoid(gate)
        active = (gate * sigma * upper).astype(LOW)
        grad_gate = grad_active * upper * sigma * (1.0 + gate * (1.0 - sigma))
        grad_upper = grad_active * gate * sigma
        grad_gu = jnp.concatenate([grad_gate.astype(LOW), grad_upper.astype(LOW)], 1)
        back = dot(grad_gu, w_gu, BY_ROWS)
        return normed, active, grad_gu, back

    near = ffn(ORDER[:3], grad_active[: 3 * mine])
    near_low = near[3].astype(LOW)
    p0 = near_low[:mine]
    came_near = [
        lax.ppermute(near_low[mine : 2 * mine], "mp", ring_shift(MP, 1)),
        lax.ppermute(near_low[2 * mine :], "mp", ring_shift(MP, 3)),
    ]
    mids[2], far_grad = after((mids[2], grad_active[3 * mine :]), near_low)
    far = ffn(ORDER[3:], far_grad)
    far_low = far[3].astype(LOW)
    came = [*came_near, lax.ppermute(far_low, "mp", ring_shift(MP, 2))]
    normed_two, active, grad_gu = [
        jnp.concatenate([a, b], 0) for a, b in zip(near[:3], far[:3])
    ]
    normed_two, active, grad_gu, grad_low = after(
        (normed_two, active, grad_gu, grad_low), far_low
    )
    ffn_part = call(
        ffn_out_kernel,
        place,
        [(active, None), (down_weight, None)],
        [((rows, width), LOW, None)],
        vmem=BIG,
    )[0]
    ffn_out = lax.psum(ffn_part, "mp")
    head_c = lax.dynamic_slice_in_dim(after(c_part, came_near[0]), natural, 8, 0)
    head_c = slab_shift(head_c, -1)
    normed_two, active_late, grad_gu, grad_low = after(
        (normed_two, active, grad_gu, grad_low), came_near[0]
    )
    block = hidden_units
    steps = 2 * hidden_units // block
    gate_up_block = pl.BlockSpec((rows, block), lambda i, s, t: (0, jnp.minimum(i, steps - 1)))
    down_block = pl.BlockSpec((rows, block), lambda i, s, t: (0, jnp.maximum(i - steps, 0)))
    ffn_grad_part = call(
        functools.partial(ffn_grad_kernel, steps),
        place,
        [(normed_two, None), (grad_gu, gate_up_block), (grad_low, None), (active_late, down_block)],
        [
            (
                (width, 3 * hidden_units),
                LOW,
                pl.BlockSpec((width, block), lambda i, s, t: (0, i)),
            )
        ],
        grid=3 * hidden_units // block,
        scratch=[pltpu.VMEM((width, rows), LOW)],
        vmem=BIG,
        flops=10**10,
    )[0]
    ffn_line = chip_line_scatter(ffn_grad_part)
    came, ffn_part, head_c, ffn_grad_part = lax.optimization_barrier(
        (tuple(came), ffn_part, head_c, ffn_grad_part)
    )
    grad_middle, grad_branch, ffn_gain_part = call(
        branch_kernel,
        place,
        [(v, None) for v in (p0, *came, middle, ffn_gain)] + [(out_grad, own_rows)],
        [quarter_full, quarter_low, ((1, width), FULL, None)],
        vmem=BIG,
    )
    branches = gather_rows(grad_branch)
    head = head_spread(grad_branch[:16])
    branches, head = lax.optimization_barrier((branches, head))

    outs = call(
        mix_back_kernel,
        place,
        [(grad_branch, None)]
        + [(branches[o], None) for o in (1, 2, 3)]
        + [
            (v, None)
            for v in (
                gated, head, head_c, b_part, c_part, x_part, convolved, tail_mixed, conv_weight,
                out_weight, w_in, normed, mix_gain, ffn_gain_part,
            )
        ],
        [((width, 4 * channels + LANES), LOW, None)]
        + [quarter_full, quarter_low, quarter_low, quarter_low],
        vmem=BIG,
        flops=10**10,
    )
    in_out_part, p0, p1, p2, p3 = outs
    in_out_line = chip_line_scatter(in_out_part)
    came = send_rows({1: p1, 2: p2, 3: p3})
    came, ffn_line, ffn_out = lax.optimization_barrier((came, ffn_line, ffn_out))
    hidden_low = call(
        hidden_kernel,
        place,
        [(v, None) for v in (p0, came[1], came[2], came[3])]
        + [(hidden_in, own_rows)]
        + [(v, None) for v in (mix_gain, grad_middle)],
        [quarter_low],
        vmem=BIG,
    )[0]
    ends = gather_rows(hidden_low)
    z = seq_place()[2]

    def along_z(line):
        line = line.reshape(Z_DIM, 32, -1)
        return [take(line, z, 0)] + [
            lax.ppermute(take(line, (z + o) % Z_DIM, 0), "seq", seq_shift(o, 0, 0))
            for o in (1, 2, 3)
        ]

    ffn_parts = along_z(after(ffn_line, hidden_low))
    in_out_line, ffn_parts = lax.optimization_barrier((after(in_out_line, ends), ffn_parts))
    lines = [*ffn_parts, *along_z(in_out_line)]
    in_done, out_done, gate_up_done, down_done, small = call(
        finish_kernel,
        place,
        [(v, None) for v in lines],
        [
            ((3, 32, channels), FULL, None),
            ((32, channels), FULL, None),
            ((2, 32, hidden_units), FULL, None),
            ((32, hidden_units), FULL, None),
            ((32, LANES), FULL, None),
        ],
    )
    gains = small[: 2 * width // LANES]
    gains = gains + sum(lax.ppermute(gains, "mp", ring_shift(MP, o)) for o in (2, 1, 3))
    gains = gains.reshape(2, width)
    taps_grad = small[2 * width // LANES : (2 * width + 3 * channels) // LANES]
    chunk = pl.BlockSpec((mine, width), lambda i, s, t: ((s[0] + i) % MP, 0))
    hidden_grad = call(
        place_kernel,
        place,
        [(v, None) for v in (hidden_low, ends[1], ends[2], ends[3])],
        [((rows, width), FULL, chunk)],
        grid=MP,
    )[0]
    hidden_out = call(
        place_add_kernel,
        place,
        [(mids[o], None) for o in range(MP)] + [(ffn_out, chunk)],
        [((rows, width), FULL, chunk)],
        grid=MP,
    )[0]
    return (
        hidden_out,
        hidden_grad,
        gains[0],
        jnp.transpose(in_done, (1, 0, 2)),
        taps_grad.reshape(3, channels),
        out_done.T,
        gains[1],
        jnp.transpose(gate_up_done, (1, 0, 2)),
        down_done.T,
    )


def solution(mesh):
    placed = (
        P("seq", None),
        P(),
        P(None, None, "mp"),
        P(None, "mp"),
        P("mp", None),
        P(),
        P(None, None, "mp"),
        P("mp", None),
        P("seq"),
        P("seq", None),
    )
    return jax.shard_map(
        on_device,
        mesh=mesh,
        in_specs=placed,
        out_specs=(
            P("seq", None),
            P("seq", None),
            P(),
            P("seq", None, "mp"),
            P(None, "mp"),
            P("mp", "seq"),
            P(),
            P("seq", None, "mp"),
            P("mp", "seq"),
        ),
        check_vma=False,
    )
```

```python
import functools
import math

import jax
import jax.numpy as jnp
from jax import lax
from jax.experimental import pallas as pl
from jax.experimental.pallas import tpu as pltpu
from jax.sharding import PartitionSpec as P

EPS = 1e-05
LOW = jnp.bfloat16
FULL = jnp.float32
MP = 4
X_DIM = 4
LANES = 128
ORDER = (0, 1, 3, 2)
Z_DIM = 4


def ring_shift(size, by):
    return [(i, (i + by) % size) for i in range(size)]


def seq_index(z, x, core):
    return (z * X_DIM + x) * 2 + core


def seq_shift(dz, dx, flip):
    return [
        (
            seq_index(z, x, core),
            seq_index((z + dz) % Z_DIM, (x + dx) % X_DIM, core ^ flip),
        )
        for z in range(Z_DIM)
        for x in range(X_DIM)
        for core in range(2)
    ]


def slab_shift(value, by):
    devices = lax.axis_size("seq")
    pairs = [(i, i + by) for i in range(devices) if 0 <= i + by < devices]
    return lax.ppermute(value, "seq", pairs)


def head_spread(value):
    devices = lax.axis_size("seq")
    came = 0
    for j in range(MP):
        pairs = [(s * MP, (s - 1) * MP + j) for s in range(1, devices)]
        came = came + lax.ppermute(value, ("seq", "mp"), pairs)
    return came


def dot(left, right, contract=((1,), (0,))):
    return lax.dot_general(left, right, (contract, ((), ())), preferred_element_type=FULL)


BY_ROWS = ((1,), (1,))
OVER_TOKENS = ((0,), (0,))


def send_rows(parts):
    return {o: lax.ppermute(parts[o], "mp", ring_shift(MP, o)) for o in (2, 1, 3)}


def gather_rows(rows, order=(2, 1, 3)):
    return {o: lax.ppermute(rows, "mp", ring_shift(MP, -o)) for o in order}


def take(value, index, axis):
    return lax.dynamic_index_in_dim(value, index, axis, keepdims=False)


def seq_place():
    me = lax.axis_index("seq")
    return me % 2, (me // 2) % X_DIM, me // (2 * X_DIM)


def chip_line_scatter(part):
    groups = [
        [seq_index(z, x, core) for x in range(X_DIM) for core in range(2)] for z in range(Z_DIM)
    ]
    return lax.psum_scatter(
        part, "seq", scatter_dimension=0, axis_index_groups=groups, tiled=True
    )


def after(values, *others):
    return lax.optimization_barrier((values, others))[0]


def turn(value, by):
    rows = value.shape[0]
    return lax.dynamic_slice_in_dim(jnp.concatenate([value, value], 0), by, rows, 0)


def inv_rms(values):
    return lax.rsqrt(jnp.mean(values * values, axis=1, keepdims=True) + EPS)


def norm_back(grad_unit, unit_rows, inv_rows):
    return inv_rows * (
        grad_unit - unit_rows * jnp.mean(grad_unit * unit_rows, axis=1, keepdims=True)
    )


def whole(shape):
    return pl.BlockSpec(shape, lambda i, s, t: (0,) * len(shape))


def quarter(o, rows, width):
    return pl.BlockSpec((rows, width), lambda i, s, t: ((s[0] + o) % MP, 0))


def call(kernel, place, inputs, outs, grid=1, vmem=0, scratch=(), flops=0):
    in_specs = [spec or whole(array.shape) for array, spec in inputs]
    out_specs = [spec or whole(shape) for shape, _, spec in outs]
    held = 0
    for (array, _), spec in zip(inputs, in_specs):
        held += math.prod(spec.block_shape) * array.dtype.itemsize
    for (_, dtype, _), spec in zip(outs, out_specs):
        held += math.prod(spec.block_shape) * jnp.dtype(dtype).itemsize
    return pl.pallas_call(
        kernel,
        grid_spec=pltpu.PrefetchScalarGridSpec(
            num_scalar_prefetch=2, grid=(grid,), in_specs=in_specs, out_specs=out_specs,
            scratch_shapes=scratch,
        ),
        out_shape=[jax.ShapeDtypeStruct(shape, dtype) for shape, dtype, _ in outs],
        compiler_params=pltpu.CompilerParams(vmem_limit_bytes=vmem or 2 * held + (8 << 20)),
        cost_estimate=pl.CostEstimate(flops=flops, bytes_accessed=0, transcendentals=0),
    )(*place, *[array for array, _ in inputs])


def places(s_ref, rows, columns):
    row = lax.broadcasted_iota(jnp.int32, (rows, columns), 0) + s_ref[0] * (rows // MP)
    return jnp.where(row >= rows, row - rows, row)


def taps(s_ref, t_ref, mixed, tail_mixed):
    rows, columns = mixed.shape
    place = places(s_ref, rows, columns)
    keep_one = place != t_ref[0]
    keep_two = keep_one & (place != t_ref[0] + 1)
    back_one = pltpu.roll(mixed, 1, 0)
    back_two = pltpu.roll(mixed, 2, 0)
    last = tail_mixed[7:8]
    before_last = tail_mixed[6:7]
    tap_one = jnp.where(keep_one, jnp.where(place == 0, last, back_one), 0.0)
    tap_two = jnp.where(
        keep_two, jnp.where(place == 0, before_last, jnp.where(place == 1, last, back_two)), 0.0
    )
    return place, keep_one, keep_two, tap_one, tap_two


def mix_kernel(
    s_ref, t_ref, h0_ref, h1_ref, h2_ref, h3_ref, tail_ref, gain_ref, w_ref, conv_ref, out_ref,
    normed_ref, b_ref, c_ref, x_ref,
    gated_ref, convolved_ref, tail_mixed_ref, p0_ref, p1_ref, p2_ref, p3_ref,
):
    gain = gain_ref[...]
    rows = p0_ref.shape[0]
    for o, ref in enumerate((h0_ref, h1_ref, h2_ref, h3_ref)):
        hidden = ref[...]
        normed_ref[o * rows : (o + 1) * rows, :] = (hidden * inv_rms(hidden) * gain).astype(LOW)
    normed = normed_ref[...]
    parts = [dot(normed, w_ref[k]) for k in range(3)]
    for part, ref in zip(parts, (b_ref, c_ref, x_ref)):
        ref[...] = part
    tail = tail_ref[...]
    tail = (tail * inv_rms(tail) * gain).astype(LOW)
    tail_mixed = (dot(tail, w_ref[0]) * dot(tail, w_ref[2])).astype(LOW).astype(FULL)
    tail_mixed_ref[...] = tail_mixed
    mixed = (parts[0] * parts[2]).astype(LOW).astype(FULL)
    _, _, _, tap_one, tap_two = taps(s_ref, t_ref, mixed, tail_mixed)
    conv = conv_ref[...]
    convolved = conv[0:1] * tap_two + conv[1:2] * tap_one + conv[2:3] * mixed
    convolved_ref[...] = convolved
    gated = (parts[1] * convolved).astype(LOW)
    gated_ref[...] = gated
    branch = dot(gated, out_ref[...])
    for o, ref in enumerate((p0_ref, p1_ref, p2_ref, p3_ref)):
        ref[...] = branch[o * rows : (o + 1) * rows].astype(ref.dtype)


def middle_kernel(s_ref, t_ref, hidden_ref, p0_ref, r1_ref, r2_ref, r3_ref, middle_ref, low_ref):
    total = hidden_ref[...] + p0_ref[...]
    for ref in (r1_ref, r2_ref, r3_ref):
        total = total + ref[...].astype(FULL)
    middle_ref[...] = total
    low_ref[...] = total.astype(LOW)


def slabs_of(part, order):
    return jnp.concatenate([part[i * 32 : (i + 1) * 32] for i in order], 0)


BIG = 60 << 20
SCATTER_ORDER = [
    seq_index(z, x, core) for x in range(X_DIM) for core in range(2) for z in range(Z_DIM)
]


def ffn_grad_kernel(
    steps, s_ref, t_ref, normed_ref, grad_gu_ref, low_ref, active_ref, part_ref, turned_ref
):
    step = pl.program_id(0)

    @pl.when(step == 0)
    def _():
        turned_ref[...] = jnp.transpose(normed_ref[...])

    @pl.when(step == steps)
    def _():
        turned_ref[...] = jnp.transpose(low_ref[...])

    @pl.when(step < steps)
    def _():
        part_ref[...] = slabs_of(dot(turned_ref[...], grad_gu_ref[...]).astype(LOW), SCATTER_ORDER)

    @pl.when(step >= steps)
    def _():
        part_ref[...] = slabs_of(dot(turned_ref[...], active_ref[...]).astype(LOW), SCATTER_ORDER)


def ffn_out_kernel(s_ref, t_ref, active_ref, down_ref, out_ref):
    part = dot(active_ref[...], down_ref[...]).astype(LOW)
    rows = part.shape[0] // MP
    for i, o in enumerate(ORDER):
        place = lax.rem(s_ref[0] + o, MP) * rows
        out_ref[pl.ds(pl.multiple_of(place, rows), rows), :] = part[i * rows : (i + 1) * rows]


def place_kernel(s_ref, t_ref, c0_ref, c1_ref, c2_ref, c3_ref, out_ref):
    for o, ref in enumerate((c0_ref, c1_ref, c2_ref, c3_ref)):

        @pl.when(pl.program_id(0) == o)
        def _():
            out_ref[...] = ref[...].astype(FULL)


def place_add_kernel(s_ref, t_ref, c0_ref, c1_ref, c2_ref, c3_ref, more_ref, out_ref):
    for o, ref in enumerate((c0_ref, c1_ref, c2_ref, c3_ref)):

        @pl.when(pl.program_id(0) == o)
        def _():
            out_ref[...] = ref[...].astype(FULL) + more_ref[...].astype(FULL)


def branch_kernel(
    s_ref, t_ref, p0_ref, r1_ref, r2_ref, r3_ref, middle_ref, gain_ref, out_grad_ref,
    grad_ref, low_ref, gain_part_ref,
):
    total = p0_ref[...].astype(FULL)
    for ref in (r1_ref, r2_ref, r3_ref):
        total = total + ref[...].astype(FULL)
    middle = middle_ref[...]
    inv = inv_rms(middle)
    unit = middle * inv
    gain_part_ref[...] = jnp.sum(total * unit, axis=0, keepdims=True)
    grad = out_grad_ref[...] + norm_back(total * gain_ref[...], unit, inv)
    grad_ref[...] = grad
    low_ref[...] = grad.astype(LOW)


def mix_back_kernel(
    s_ref, t_ref, g0_ref, g1_ref, g2_ref, g3_ref, gated_ref, head_ref, head_c_ref, b_ref, c_ref, x_ref,
    convolved_ref, tail_mixed_ref, conv_ref, out_ref, w_ref, normed_ref, gain_ref,
    ffn_gain_ref, part_ref, p0_ref, p1_ref, p2_ref, p3_ref,
):
    out_weight = out_ref[...]
    conv = conv_ref[...]
    grad_gated = jnp.concatenate(
        [dot(ref[...], out_weight, BY_ROWS) for ref in (g0_ref, g1_ref, g2_ref, g3_ref)], 0
    )
    head = dot(head_ref[...], out_weight, BY_ROWS)[:8] * head_c_ref[...]
    came_before_last = conv[0:1] * head[0:1]
    came_last = conv[0:1] * head[1:2] + conv[1:2] * head[0:1]
    b_part, c_part, x_part = b_ref[...], c_ref[...], x_ref[...]
    mixed = (b_part * x_part).astype(LOW).astype(FULL)
    place, keep_one, keep_two, tap_one, tap_two = taps(s_ref, t_ref, mixed, tail_mixed_ref[...])
    rows = mixed.shape[0]
    grad_conv = grad_gated * c_part
    conv_part = [
        jnp.sum(grad_conv * tap, axis=0, keepdims=True) for tap in (tap_two, tap_one, mixed)
    ]
    to_one = jnp.where(keep_one, conv[1:2] * grad_conv, 0.0)
    to_two = jnp.where(keep_two, conv[0:1] * grad_conv, 0.0)
    from_one = pltpu.roll(to_one, rows - 1, 0)
    from_two = pltpu.roll(to_two, rows - 2, 0)
    is_last, is_before_last = place == rows - 1, place == rows - 2
    grad_mixed = (
        conv[2:3] * grad_conv
        + jnp.where(is_last, came_last, from_one)
        + jnp.where(is_last, 0.0, jnp.where(is_before_last, came_before_last, from_two))
    )
    grad_mixed = grad_mixed.astype(LOW).astype(FULL)
    grads = [
        (grad_mixed * x_part).astype(LOW),
        (grad_gated * convolved_ref[...]).astype(LOW),
        (grad_mixed * b_part).astype(LOW),
    ]
    columns = mixed.shape[1]
    turned = jnp.transpose(normed_ref[...])
    for k, grad in enumerate(grads):
        part_ref[:, k * columns : (k + 1) * columns] = slabs_of(
            dot(turned, grad).astype(LOW), SCATTER_ORDER
        )
    branch = jnp.concatenate([ref[...] for ref in (g0_ref, g1_ref, g2_ref, g3_ref)], 0)
    part_ref[:, 3 * columns : 4 * columns] = slabs_of(
        dot(jnp.transpose(branch), gated_ref[...]).astype(LOW), SCATTER_ORDER
    )
    quarter_rows = rows // MP
    sends = (p0_ref, p1_ref, p2_ref, p3_ref)
    gain_part = 0.0
    for o, ref in enumerate(sends):
        cut = slice(o * quarter_rows, (o + 1) * quarter_rows)
        part = sum(dot(grads[k][cut], w_ref[k], BY_ROWS) for k in range(3))
        ref[...] = part.astype(ref.dtype)
        gain_part = gain_part + jnp.sum(
            part * normed_ref[cut, :].astype(FULL), axis=0, keepdims=True
        )
    conv_row = jnp.concatenate([*conv_part, jnp.zeros_like(conv_part[0])], 1)
    small = [gain_part / gain_ref[...], ffn_gain_ref[...], conv_row]
    lanes = part_ref.shape[1] - 4 * columns
    pieces = [row[:, i : i + lanes] for row in small for i in range(0, row.shape[1], lanes)]
    tile = jnp.concatenate([*pieces, jnp.zeros((8, lanes), FULL)], 0).astype(LOW)
    part_ref[:, 4 * columns :] = jnp.concatenate([tile] * (part_ref.shape[0] // 32), 0)


def hidden_kernel(
    s_ref, t_ref, p0_ref, r1_ref, r2_ref, r3_ref, hidden_ref, gain_ref, grad_ref, low_ref
):
    total = p0_ref[...]
    for ref in (r1_ref, r2_ref, r3_ref):
        total = total + ref[...].astype(FULL)
    hidden = hidden_ref[...]
    inv = inv_rms(hidden)
    grad = grad_ref[...] + norm_back(total * gain_ref[...], hidden * inv, inv)
    low_ref[...] = grad.astype(LOW)


def finish_kernel(s_ref, t_ref, *refs):
    in_ref, out_ref, gate_up_ref, down_ref, small_ref = refs[8:]

    def total(parts, start, size):
        return sum(ref[:, start : start + size].astype(FULL) for ref in parts)

    ffn_parts, mix_parts = refs[:4], refs[4:8]
    units = down_ref.shape[1]
    channels = out_ref.shape[1]
    for k in range(2):
        gate_up_ref[k] = total(ffn_parts, k * units, units)
    down_ref[...] = total(ffn_parts, 2 * units, units)
    for k in range(3):
        in_ref[k] = total(mix_parts, k * channels, channels)
    out_ref[...] = total(mix_parts, 3 * channels, channels)
    small_ref[...] = total(mix_parts, 4 * channels, LANES)


def on_device(
    hidden_in,
    mix_gain,
    in_weight,
    conv_weight,
    out_weight,
    ffn_gain,
    gate_up_weight,
    down_weight,
    seq_starts,
    out_grad,
):
    rows, width = hidden_in.shape
    mine = rows // MP
    channels = conv_weight.shape[1]
    hidden_units = down_weight.shape[0]
    me = lax.axis_index("mp")
    start = me * mine
    natural = (rows - start) % rows
    place = (me.astype(jnp.int32)[None], seq_starts)
    mix_gain = mix_gain[None]
    ffn_gain = ffn_gain[None]
    w_in = jnp.transpose(in_weight, (1, 0, 2))
    w_gu = jnp.transpose(gate_up_weight, (1, 0, 2))
    own_rows = quarter(0, mine, width)

    tail_in = slab_shift(hidden_in[rows - 8 :], 1)
    quarter_low = ((mine, width), LOW, None)
    quarter_full = ((mine, width), FULL, None)
    low_part = ((rows, channels), LOW, None)
    full_part = ((rows, channels), FULL, None)
    outs = call(
        mix_kernel,
        place,
        [(hidden_in, quarter(o, mine, width)) for o in range(MP)]
        + [(v, None) for v in (tail_in, mix_gain, w_in, conv_weight, out_weight)],
        [((rows, width), LOW, None), full_part, full_part, full_part]
        + [low_part, full_part, ((8, channels), FULL, None)]
        + [quarter_full, quarter_low, quarter_low, quarter_low],
        vmem=BIG,
    )
    normed, b_part, c_part, x_part, gated, convolved, tail_mixed, p0, p1, p2, p3 = outs
    came = send_rows({1: p1, 2: p2, 3: p3})
    w_gu = after(gate_up_weight, came[1]).reshape(width, -1)
    came, w_gu = lax.optimization_barrier((came, w_gu))
    middle, middle_low = call(
        middle_kernel,
        place,
        [(hidden_in, own_rows), (p0, None), (came[1], None), (came[2], None), (came[3], None)],
        [quarter_full, quarter_low],
    )
    mids = {0: middle_low, **gather_rows(middle_low, (1, 3, 2))}
    late_grad = after(out_grad, middle_low)
    grad_low = jnp.concatenate(
        [lax.dynamic_slice_in_dim(late_grad, ((me + o) % MP) * mine, mine, 0) for o in ORDER], 0
    ).astype(LOW)
    grad_active = dot(grad_low, down_weight, BY_ROWS)
    mids[1], mids[3], grad_active = lax.optimization_barrier((mids[1], mids[3], grad_active))

    def ffn(offsets, grad_active):
        middle = jnp.concatenate([mids[o] for o in offsets], 0).astype(FULL)
        normed = (middle * inv_rms(middle) * ffn_gain).astype(LOW)
        gate_up = dot(normed, w_gu)
        gate, upper = gate_up[:, :hidden_units], gate_up[:, hidden_units:]
        sigma = jax.nn.sigmoid(gate)
        active = (gate * sigma * upper).astype(LOW)
        grad_gate = grad_active * upper * sigma * (1.0 + gate * (1.0 - sigma))
        grad_upper = grad_active * gate * sigma
        grad_gu = jnp.concatenate([grad_gate.astype(LOW), grad_upper.astype(LOW)], 1)
        back = dot(grad_gu, w_gu, BY_ROWS)
        return normed, active, grad_gu, back

    near = ffn(ORDER[:3], grad_active[: 3 * mine])
    near_low = near[3].astype(LOW)
    p0 = near_low[:mine]
    came_near = [
        lax.ppermute(near_low[mine : 2 * mine], "mp", ring_shift(MP, 1)),
        lax.ppermute(near_low[2 * mine :], "mp", ring_shift(MP, 3)),
    ]
    mids[2], far_grad = after((mids[2], grad_active[3 * mine :]), near_low)
    far = ffn(ORDER[3:], far_grad)
    far_low = far[3].astype(LOW)
    came = [*came_near, lax.ppermute(far_low, "mp", ring_shift(MP, 2))]
    normed_two, active, grad_gu = [
        jnp.concatenate([a, b], 0) for a, b in zip(near[:3], far[:3])
    ]
    normed_two, active, grad_gu, grad_low = after(
        (normed_two, active, grad_gu, grad_low), far_low
    )
    ffn_part = call(
        ffn_out_kernel,
        place,
        [(active, None), (down_weight, None)],
        [((rows, width), LOW, None)],
        vmem=BIG,
    )[0]
    ffn_out = lax.psum(ffn_part, "mp")
    head_c = lax.dynamic_slice_in_dim(after(c_part, came_near[0]), natural, 8, 0)
    head_c = slab_shift(head_c, -1)
    normed_two, active_late, grad_gu, grad_low = after(
        (normed_two, active, grad_gu, grad_low), came_near[0]
    )
    block = hidden_units
    steps = 2 * hidden_units // block
    gate_up_block = pl.BlockSpec((rows, block), lambda i, s, t: (0, jnp.minimum(i, steps - 1)))
    down_block = pl.BlockSpec((rows, block), lambda i, s, t: (0, jnp.maximum(i - steps, 0)))
    ffn_grad_part = call(
        functools.partial(ffn_grad_kernel, steps),
        place,
        [(normed_two, None), (grad_gu, gate_up_block), (grad_low, None), (active_late, down_block)],
        [
            (
                (width, 3 * hidden_units),
                LOW,
                pl.BlockSpec((width, block), lambda i, s, t: (0, i)),
            )
        ],
        grid=3 * hidden_units // block,
        scratch=[pltpu.VMEM((width, rows), LOW)],
        vmem=BIG,
        flops=10**10,
    )[0]
    ffn_line = chip_line_scatter(ffn_grad_part)
    came, ffn_part, head_c, ffn_grad_part = lax.optimization_barrier(
        (tuple(came), ffn_part, head_c, ffn_grad_part)
    )
    grad_middle, grad_branch, ffn_gain_part = call(
        branch_kernel,
        place,
        [(v, None) for v in (p0, *came, middle, ffn_gain)] + [(out_grad, own_rows)],
        [quarter_full, quarter_low, ((1, width), FULL, None)],
        vmem=BIG,
    )
    branches = gather_rows(grad_branch)
    head = head_spread(grad_branch[:16])
    branches, head = lax.optimization_barrier((branches, head))

    outs = call(
        mix_back_kernel,
        place,
        [(grad_branch, None)]
        + [(branches[o], None) for o in (1, 2, 3)]
        + [
            (v, None)
            for v in (
                gated, head, head_c, b_part, c_part, x_part, convolved, tail_mixed, conv_weight,
                out_weight, w_in, normed, mix_gain, ffn_gain_part,
            )
        ],
        [((width, 4 * channels + LANES), LOW, None)]
        + [quarter_full, quarter_low, quarter_low, quarter_low],
        vmem=BIG,
        flops=10**10,
    )
    in_out_part, p0, p1, p2, p3 = outs
    in_out_line = chip_line_scatter(in_out_part)
    came = send_rows({1: p1, 2: p2, 3: p3})
    came, ffn_line, ffn_out = lax.optimization_barrier((came, ffn_line, ffn_out))
    hidden_low = call(
        hidden_kernel,
        place,
        [(v, None) for v in (p0, came[1], came[2], came[3])]
        + [(hidden_in, own_rows)]
        + [(v, None) for v in (mix_gain, grad_middle)],
        [quarter_low],
        vmem=BIG,
    )[0]
    ends = gather_rows(hidden_low)
    z = seq_place()[2]

    def along_z(line):
        line = line.reshape(Z_DIM, 32, -1)
        return [take(line, z, 0)] + [
            lax.ppermute(take(line, (z + o) % Z_DIM, 0), "seq", seq_shift(o, 0, 0))
            for o in (1, 2, 3)
        ]

    chunk = pl.BlockSpec((mine, width), lambda i, s, t: ((s[0] + i) % MP, 0))
    hidden_grad = call(
        place_kernel,
        place,
        [(v, None) for v in (hidden_low, ends[1], ends[2], ends[3])],
        [((rows, width), FULL, chunk)],
        grid=MP,
    )[0]
    hidden_out = call(
        place_add_kernel,
        place,
        [(mids[o], None) for o in range(MP)] + [(ffn_out, chunk)],
        [((rows, width), FULL, chunk)],
        grid=MP,
    )[0]
    ffn_parts = along_z(after(ffn_line, hidden_low))
    in_out_line, ffn_parts = lax.optimization_barrier((after(in_out_line, hidden_grad, hidden_out), ffn_parts))
    lines = [*ffn_parts, *along_z(in_out_line)]
    in_done, out_done, gate_up_done, down_done, small = call(
        finish_kernel,
        place,
        [(v, None) for v in lines],
        [
            ((3, 32, channels), FULL, None),
            ((32, channels), FULL, None),
            ((2, 32, hidden_units), FULL, None),
            ((32, hidden_units), FULL, None),
            ((32, LANES), FULL, None),
        ],
    )
    gains = small[: 2 * width // LANES]
    gains = gains + sum(lax.ppermute(gains, "mp", ring_shift(MP, o)) for o in (2, 1, 3))
    gains = gains.reshape(2, width)
    taps_grad = small[2 * width // LANES : (2 * width + 3 * channels) // LANES]
    return (
        hidden_out,
        hidden_grad,
        gains[0],
        jnp.transpose(in_done, (1, 0, 2)),
        taps_grad.reshape(3, channels),
        out_done.T,
        gains[1],
        jnp.transpose(gate_up_done, (1, 0, 2)),
        down_done.T,
    )


def solution(mesh):
    placed = (
        P("seq", None),
        P(),
        P(None, None, "mp"),
        P(None, "mp"),
        P("mp", None),
        P(),
        P(None, None, "mp"),
        P("mp", None),
        P("seq"),
        P("seq", None),
    )
    return jax.shard_map(
        on_device,
        mesh=mesh,
        in_specs=placed,
        out_specs=(
            P("seq", None),
            P("seq", None),
            P(),
            P("seq", None, "mp"),
            P(None, "mp"),
            P("mp", "seq"),
            P(),
            P("seq", None, "mp"),
            P("mp", "seq"),
        ),
        check_vma=False,
    )
```
